256 devices in a mesh: ctx: 32 (over z, y), head: 8 (over x, core).
Axes of the slice: x: 4, y: 4, z: 8, core: 2. Of those that a mesh axis runs over, the one named last changes fastest.
Arguments:
- latents: float32 [512, 1024], replicated, may hold values from -5 to 5
- observations: float32 [65536, 1024], P('ctx'), may hold values from -45 to 45
- w_query: float32 [1024, 1024], P(None, 'head'), as said below
- w_key: float32 [1024, 1024], P(None, 'head'), as said below
- w_value: float32 [1024, 1024], P(None, 'head'), may hold values from -0.1875 to 0.1875
- w_out: float32 [1024, 1024], P('head'), may hold values from -0.1875 to 0.1875
- d_out: float32 [512, 1024], replicated, may hold values from -6 to 6
Outputs:
- d_latents: float32 [512, 1024], P(None, 'head')
- d_observations: float32 [65536, 1024], P('ctx', 'head')
- d_w_query: float32 [1024, 1024], P(None, 'head')
- d_w_key: float32 [1024, 1024], P('ctx', 'head')
- d_w_value: float32 [1024, 1024], P('ctx', 'head')
- d_w_out: float32 [1024, 1024], P('head')
The draws below stay inside these ranges and needn't reach their ends.
Inputs may be any that keep to these rules, and one draw needn't show every extreme that they name: `w_query`: every entry lies within -5 / sqrt(1024) to 5 / sqrt(1024). `w_key`: every entry lies within -7 / sqrt(1024) to 7 / sqrt(1024).
All inputs are finite; a program needn't handle non-finite values.
Results may differ from the reference program's by a relative error of at most 0.0003.
Values sent between devices are 32-bit elements; how exact they have to be, the bound alone decides.
No kernel may reach another device: no remote copies, remote signals or barrier semaphores. Data moves between devices by JAX's collectives and lax.ppermute only.
A program may use at most 128 MiB of HBM per device.

```python
import math
import jax
import jax.numpy as jnp
from jax import lax

D = 1024
HEADS = 8
DH = 128
LAT = 512
TOKENS = 65536


def shared_latents(key):
    return jnp.clip(jax.random.normal(key, (LAT, D), jnp.float32), -5.0, 5.0)


def shared_query(key):
    base = jax.random.normal(jax.random.fold_in(key, 100), (D, HEADS * DH), jnp.float32)
    return jnp.clip(base, -5.0, 5.0) / jnp.sqrt(jnp.float32(D))


def draw_latents(key, part):
    drawn = shared_latents(key)
    return drawn


def draw_observations(key, part):
    key = jax.random.fold_in(key, 2)
    return jnp.clip(jax.random.normal(key, (TOKENS, D), jnp.float32), -5.0, 5.0)


def draw_w_query(key, part):
    return shared_query(key)


def draw_w_key(key, part):
    key = jax.random.fold_in(key, 3)
    own = jnp.clip(jax.random.normal(key, (D, HEADS * DH), jnp.float32), -5.0, 5.0) / jnp.sqrt(jnp.float32(D))
    return own


def levels(own_key, shape, split, least, largest):
    factor_of, own = 1.0, jax.random.fold_in(own_key, 6)
    for dim, parts in split:
        steps = jnp.exp(jax.random.uniform(jax.random.fold_in(own, dim), (parts,), jnp.float32, least / len(split), largest / len(split)))
        factor_of = factor_of * jnp.repeat(steps, shape[dim] // parts).reshape([-1 if axis == dim else 1 for axis in range(len(shape))])
    return factor_of


def bell_draw(rng, dims, scale, reach, shards=(), kind=jnp.bfloat16):
    array = jax.random.normal(rng, dims, jnp.float32) * scale
    if len(shards) > 0:
        array = levels(rng, dims, shards, -0.22, 0.18) * array
    return jnp.clip(array, min=-reach, max=reach).astype(kind)


def setup_inputs(seed: int = 0) -> dict:
    key_of = jax.random.split(jax.random.key(seed), 8)
    return {
        "latents": draw_latents(jax.random.fold_in(key_of[7], 71), 0),
        "observations": draw_observations(jax.random.fold_in(key_of[7], 71), 0),
        "w_query": draw_w_query(jax.random.fold_in(key_of[7], 71), 0),
        "w_key": draw_w_key(jax.random.fold_in(key_of[7], 71), 0),
        "w_value": bell_draw(key_of[4], (D, HEADS * DH), D ** -0.5, 0.1875, ((1, 8),), jnp.float32),
        "w_out": bell_draw(key_of[5], (HEADS * DH, D), (HEADS * DH) ** -0.5, 0.1875, ((0, 8),), jnp.float32),
        "d_out": bell_draw(key_of[6], (LAT, D), 1.0, 6.0, (), jnp.float32),
    }


def reference(latents, observations, w_query, w_key, w_value, w_out, d_out):
    highest = lax.Precision.HIGHEST
    scale = 1.0 / math.sqrt(DH)
    queries = jnp.dot(latents, w_query, precision=highest, preferred_element_type=jnp.float32).reshape(LAT, HEADS, DH)
    keys_all = jnp.dot(observations, w_key, precision=highest, preferred_element_type=jnp.float32).reshape(TOKENS, HEADS, DH)
    values_all = jnp.dot(observations, w_value, precision=highest, preferred_element_type=jnp.float32).reshape(TOKENS, HEADS, DH)
    grad_heads = jnp.dot(d_out, w_out.T, precision=highest, preferred_element_type=jnp.float32).reshape(LAT, HEADS, DH)

    def one_head(pieces):
        query_h, key_h, value_h, grad_h = pieces
        scores = jnp.dot(query_h, key_h.T, precision=highest, preferred_element_type=jnp.float32) * scale
        probs = jnp.exp(scores - lax.optimization_barrier(jnp.max(scores, axis=1, keepdims=True)))
        probs = probs / lax.optimization_barrier(jnp.sum(probs, axis=1, keepdims=True))
        attended = jnp.dot(probs, value_h, precision=highest, preferred_element_type=jnp.float32)
        dprobs = jnp.dot(grad_h, value_h.T, precision=highest, preferred_element_type=jnp.float32)
        delta = lax.optimization_barrier(jnp.sum(grad_h * attended, axis=1, keepdims=True))
        dscores = probs * (dprobs - delta) * scale
        dquery = jnp.dot(dscores, key_h, precision=highest, preferred_element_type=jnp.float32)
        dkey = jnp.dot(dscores.T, query_h, precision=highest, preferred_element_type=jnp.float32)
        dvalue = jnp.dot(probs.T, grad_h, precision=highest, preferred_element_type=jnp.float32)
        return (attended, dquery, dkey, dvalue)
    stacked = (jnp.transpose(queries, (1, 0, 2)), jnp.transpose(keys_all, (1, 0, 2)), jnp.transpose(values_all, (1, 0, 2)), jnp.transpose(grad_heads, (1, 0, 2)))
    attended, dquery, dkey, dvalue = lax.map(one_head, stacked)
    attended = jnp.transpose(attended, (1, 0, 2)).reshape(LAT, HEADS * DH)
    dquery = jnp.transpose(dquery, (1, 0, 2)).reshape(LAT, HEADS * DH)
    dkey = jnp.transpose(dkey, (1, 0, 2)).reshape(TOKENS, HEADS * DH)
    dvalue = jnp.transpose(dvalue, (1, 0, 2)).reshape(TOKENS, HEADS * DH)
    d_w_out = jnp.dot(attended.T, d_out, precision=highest, preferred_element_type=jnp.float32)
    d_latents = jnp.dot(dquery, w_query.T, precision=highest, preferred_element_type=jnp.float32)
    d_w_query = jnp.dot(latents.T, dquery, precision=highest, preferred_element_type=jnp.float32)
    d_observations = jnp.dot(dkey, w_key.T, precision=highest, preferred_element_type=jnp.float32) + jnp.dot(dvalue, w_value.T, precision=highest, preferred_element_type=jnp.float32)
    d_w_key = jnp.dot(observations.T, dkey, precision=highest, preferred_element_type=jnp.float32)
    d_w_value = jnp.dot(observations.T, dvalue, precision=highest, preferred_element_type=jnp.float32)
    return (d_latents, d_observations, d_w_query, d_w_key, d_w_value, d_w_out)
```

```python
import math

import jax
import jax.numpy as jnp
from jax import lax
from jax.experimental import pallas as pl
from jax.experimental.pallas import tpu as pltpu
from jax.sharding import PartitionSpec as P

DH = 128
NY = 4
CHUNK = 512
F32 = jnp.float32
BF16 = jnp.bfloat16
VMEM = pltpu.VMEM
WHOLE = pl.BlockSpec(memory_space=VMEM)
ANY = pl.BlockSpec(memory_space=pl.ANY)
HBM = pl.BlockSpec(memory_space=pltpu.HBM)
SCALARS = pl.BlockSpec(memory_space=pltpu.SMEM)


def shape(*dims, dtype=F32):
    return jax.ShapeDtypeStruct(dims, dtype)


def params(mib):
    return pltpu.CompilerParams(vmem_limit_bytes=mib << 20)


def cost(macs, bytes_accessed):
    return pl.CostEstimate(flops=6 * macs, bytes_accessed=bytes_accessed, transcendentals=0)


def mm(a, b, ca=1, cb=0):
    return lax.dot_general(a, b, (((ca,), (cb,)), ((), ())), preferred_element_type=F32)


def split(a):
    hi = a.astype(BF16)
    return hi, (a - hi.astype(F32)).astype(BF16)


def dot3(a, b, ca=1, cb=0):
    a_hi, a_lo = split(a)
    b_hi, b_lo = split(b)
    return mm(a_hi, b_hi, ca, cb) + mm(a_hi, b_lo, ca, cb) + mm(a_lo, b_hi, ca, cb)


def scores_of(kv_ref, q3, g3):
    hi_k, hi_v, lo_k, lo_v = (kv_ref[:, i * DH : (i + 1) * DH] for i in range(4))
    scores = mm(jnp.concatenate([hi_k, lo_k, hi_k], axis=1), q3[...], 1, 1)
    return scores, mm(jnp.concatenate([hi_v, lo_v, hi_v], axis=1), g3[...], 1, 1)


def forward_kernel(
    scale, core_ref, lat_hbm, dout_hbm, wq_hbm, wo_hbm, wk_hbm, wv_hbm, obs_hbm,
    kv_ref, q3, g3, sent_ref, stat_ref, given_ref,
    lat_v, dout_v, wq_v, wo_v, wk_v, wv_v, obs_v, sems, obs_sems, w_hi, w_lo,
):
    step = pl.program_id(0)
    loads = [
        pltpu.make_async_copy(source, target, sems.at[i])
        for i, (source, target) in enumerate(
            (
                (wk_hbm, wk_v), (wv_hbm, wv_v), (lat_hbm, lat_v),
                (wq_hbm, wq_v), (dout_hbm, dout_v), (wo_hbm, wo_v),
            )
        )
    ]

    def load_tokens(i):
        rows = pl.ds(pl.multiple_of(i * CHUNK, CHUNK), CHUNK)
        return pltpu.make_async_copy(obs_hbm.at[rows], obs_v.at[i], obs_sems.at[i])

    @pl.when(step == 0)
    def _():
        loads[0].start()
        loads[1].start()
        load_tokens(0).start()
        for load in loads[2:]:
            load.start()
        for i in range(1, obs_v.shape[0]):
            load_tokens(i).start()
        loads[0].wait()
        loads[1].wait()
        hi, lo = split(wk_v[...])
        w_hi[:, :DH], w_lo[:, :DH] = hi, lo
        hi, lo = split(wv_v[...])
        w_hi[:, DH:], w_lo[:, DH:] = hi, lo
        for d in range(given_ref.shape[0]):
            at = pl.ds(pl.multiple_of((2 * d + 1 - core_ref[0]) * DH, DH), DH)
            given_ref[d, :, :DH], given_ref[d, :, DH:] = wk_v[at], wv_v[at]

    load_tokens(step).wait()
    o_hi, o_lo = split(obs_v[step])
    kv = mm(o_hi, w_hi[...]) + mm(o_hi, w_lo[...]) + mm(o_lo, w_hi[...])
    hi, lo = split(kv)
    kv_ref[:, : 2 * DH], kv_ref[:, 2 * DH :] = hi, lo

    @pl.when(step == 0)
    def _():
        loads[2].wait()
        loads[3].wait()
        top, bottom = split(dot3(lat_v[...], wq_v[...]) * scale)
        q3[:, :DH], q3[:, DH : 2 * DH], q3[:, 2 * DH :] = top, top, bottom
        loads[4].wait()
        loads[5].wait()
        top, bottom = split(dot3(dout_v[...], wo_v[...], 1, 1))
        g3[:, :DH], g3[:, DH : 2 * DH], g3[:, 2 * DH :] = top, top, bottom

    scores, dprobs = scores_of(kv_ref, q3, g3)
    top = jnp.max(scores, axis=0, keepdims=True)
    expo = jnp.exp(scores - top)
    total = jnp.sum(expo, axis=0, keepdims=True)
    mix = jnp.sum(expo * dprobs, axis=0, keepdims=True)

    @pl.when(step == 0)
    def _():
        stat_ref[0:1], stat_ref[1:2], stat_ref[2:3] = top, total, mix

    @pl.when(step > 0)
    def _():
        before = stat_ref[0:1]
        now = jnp.maximum(before, top)
        w_before, w_new = jnp.exp(before - now), jnp.exp(top - now)
        stat_ref[0:1] = now
        stat_ref[1:2] = stat_ref[1:2] * w_before + total * w_new
        stat_ref[2:3] = stat_ref[2:3] * w_before + mix * w_new

    @pl.when(step == pl.num_programs(0) - 1)
    def _():
        sent_ref[...] = jnp.broadcast_to(stat_ref[...][None], sent_ref.shape)


def forward(n_ctx, core, latents, d_out, w_query, w_out, w_key, w_value, observations):
    lat, tok, width = latents.shape[0], observations.shape[0], observations.shape[1]
    steps = tok // CHUNK
    nx = width // DH // 2
    block = lambda cols: pl.BlockSpec((CHUNK, cols), lambda i: (i, 0))
    full = lambda *dims: pl.BlockSpec(dims, lambda i: (0,) * len(dims))
    return pl.pallas_call(
        lambda *refs: forward_kernel(1.0 / math.sqrt(DH), *refs),
        grid=(steps,),
        in_specs=[SCALARS] + [HBM] * 7,
        out_specs=[
            block(4 * DH), full(lat, 3 * DH), full(lat, 3 * DH),
            full(n_ctx, 3, lat), full(3, lat), full(nx, DH, 2 * DH),
        ],
        out_shape=[
            shape(tok, 4 * DH, dtype=BF16),
            shape(lat, 3 * DH, dtype=BF16), shape(lat, 3 * DH, dtype=BF16),
            shape(n_ctx, 3, lat), shape(3, lat), shape(nx, DH, 2 * DH),
        ],
        scratch_shapes=[
            VMEM(latents.shape, F32), VMEM(d_out.shape, F32), VMEM(w_query.shape, F32),
            VMEM(w_out.shape, F32), VMEM(w_key.shape, F32), VMEM(w_value.shape, F32),
            VMEM((steps, CHUNK, width), F32),
            pltpu.SemaphoreType.DMA((6,)), pltpu.SemaphoreType.DMA((steps,)),
            VMEM((width, 2 * DH), BF16), VMEM((width, 2 * DH), BF16),
        ],
        compiler_params=params(60),
        cost_estimate=cost(tok * width * 256 + 2 * tok * lat * DH, 18 << 20),
        name="forward",
    )(core, latents, d_out, w_query, w_out, w_key, w_value, observations)


def sums_kernel(y_ref, kv_ref, q3, g3, stat_ref, o0, o1, o2, o3, acc):
    step = pl.program_id(0)
    stat = stat_ref[...]
    shift = stat[2:3] / stat[1:2]
    scores, dprobs = scores_of(kv_ref, q3, g3)
    expo = jnp.exp(scores - stat[0:1])
    mixed = expo * (dprobs - shift)
    kv = kv_ref[...]
    hi, lo = kv[:, : 2 * DH], kv[:, 2 * DH :]
    e_hi, e_lo = split(expo)
    m_hi, m_lo = split(mixed)
    kv_sums = mm(hi, e_hi, 0, 0) + mm(lo, e_hi, 0, 0) + mm(hi, e_lo, 0, 0)
    k_hi, k_lo = hi[:, :DH], lo[:, :DH]
    ak_sums = mm(k_hi, m_hi, 0, 0) + mm(k_lo, m_hi, 0, 0) + mm(k_hi, m_lo, 0, 0)

    @pl.when(step == 0)
    def _():
        acc[:DH], acc[DH:] = ak_sums, kv_sums

    @pl.when(step > 0)
    def _():
        acc[:DH] += ak_sums
        acc[DH:] += kv_sums

    @pl.when(step == pl.num_programs(0) - 1)
    def _():
        rows = o0.shape[0]
        for k, out in enumerate((o0, o1, o2, o3)):
            at = lax.rem(y_ref[0] + k, NY) * rows
            out[...] = acc[:, pl.ds(pl.multiple_of(at, rows), rows)].T


def local_sums(y, kv, q3, g3, stat):
    tok, lat = kv.shape[0], q3.shape[0]
    block = lambda cols: pl.BlockSpec((CHUNK, cols), lambda i: (i, 0))
    rows = lat // NY
    return pl.pallas_call(
        sums_kernel,
        grid=(tok // CHUNK,),
        in_specs=[SCALARS, block(4 * DH), WHOLE, WHOLE, WHOLE],
        out_specs=[pl.BlockSpec((rows, 3 * DH), lambda i: (0, 0))] * NY,
        out_shape=[shape(rows, 3 * DH)] * NY,
        scratch_shapes=[VMEM((3 * DH, lat), F32)],
        compiler_params=params(24),
        cost_estimate=cost(3 * tok * lat * DH, 12 << 20),
        name="local_sums",
    )(y, kv, q3, g3, stat)


def grads_kernel(kv_ref, q3, g3, stat_ref, out_ref):
    stat = stat_ref[...]
    scores, dprobs = scores_of(kv_ref, q3, g3)
    probs = jnp.exp(scores - stat[0:1]) * stat[1:2]
    dscores = probs * (dprobs - stat[2:3])
    for at, value, packed in ((0, dscores, q3), (DH, probs, g3)):
        hi, lo = split(value)
        both = mm(hi, packed[:, DH:])
        out_ref[:, at : at + DH] = both[:, :DH] + both[:, DH:] + mm(lo, packed[:, :DH])


def token_grads(half, kv, q3, g3, stat):
    tok, lat = kv.shape[0], q3.shape[0]
    steps = tok // CHUNK // 2
    first = half * steps
    return pl.pallas_call(
        grads_kernel,
        grid=(steps,),
        in_specs=[
            pl.BlockSpec((CHUNK, 4 * DH), lambda i: (i + first, 0)), WHOLE, WHOLE, WHOLE,
        ],
        out_specs=pl.BlockSpec((CHUNK, 2 * DH), lambda i: (i, 0)),
        out_shape=shape(tok // 2, 2 * DH),
        compiler_params=params(24),
        cost_estimate=cost(2 * tok * lat * DH, 5 << 20),
        name="token_grads",
    )(kv, q3, g3, stat)


def project(own, other, w):
    o_hi, o_lo = split(own)
    t_hi, t_lo = split(other)
    hi = jnp.concatenate([o_hi, t_hi], axis=1)
    lo = jnp.concatenate([o_lo, t_lo], axis=1)
    both = mm(hi, w, 1, 1)
    return both[:, :DH] + both[:, DH:] + mm(lo, w[:DH], 1, 1)


def first_kernel(*refs):
    after, own_a, other_a, own_b, other_b, far, near, back, right_ref, left_ref = refs
    a, b = (own_a[...], other_a[...]), (own_b[...], other_b[...])
    right_ref[0] = project(*a, far[0])
    right_ref[1] = project(*b, near[0])
    left_ref[0] = project(*b, far[0])
    left_ref[1] = project(*a, back[0])


def second_kernel(after, own_a, other_a, own_b, other_b, near, back, ra, la, right_ref, left_ref):
    right_ref[...] = project(own_a[...], other_a[...], near[0]) + ra[0]
    left_ref[...] = project(own_b[...], other_b[...], back[0]) + la[0]


def token_part(kernel, a, b, w, which, after, extras, outs, name):
    rows = a[0].shape[0]
    block = pl.BlockSpec((CHUNK, 2 * DH), lambda i: (i, 0))
    pair = pl.BlockSpec((2, CHUNK, DH), lambda i: (0, i, 0))
    one = pl.BlockSpec((CHUNK, DH), lambda i: (i, 0))
    chosen = [pl.BlockSpec((1,) + w.shape[1:], lambda i, k=k: (k, 0, 0)) for k in which]
    return pl.pallas_call(
        kernel,
        grid=(rows // CHUNK,),
        in_specs=[ANY] + [block] * 4 + chosen
        + [pl.BlockSpec((1, CHUNK, DH), lambda i: (0, i, 0))] * len(extras),
        out_specs=[pair if len(o.shape) == 3 else one for o in outs],
        out_shape=outs,
        compiler_params=params(24),
        cost_estimate=cost(4 * rows * 4 * DH * DH, 6 << 20),
        name=name,
    )(after, *a, *b, *[w] * len(which), *extras)


def last_kernel(own_a, other_a, own_b, other_b, w, right1, left1, right2, left2, out_ref):
    step = pl.program_id(0)

    @pl.when(step < pl.num_programs(0) // 2)
    def _():
        out_ref[...] = project(own_a[...], other_a[...], w[0]) + right2[...] + left1[0]

    @pl.when(step >= pl.num_programs(0) // 2)
    def _():
        out_ref[...] = project(own_b[...], other_b[...], w[0]) + right1[0] + left2[...]


def token_last(a, b, w, right1, left1, right2, left2):
    rows = a[0].shape[0]
    steps = rows // CHUNK
    early = lambda i: jnp.minimum(i, steps - 1)
    late = lambda i: jnp.maximum(i - steps, 0)
    first = lambda cols: pl.BlockSpec((CHUNK, cols), lambda i: (early(i), 0))
    second = lambda cols: pl.BlockSpec((CHUNK, cols), lambda i: (late(i), 0))
    return pl.pallas_call(
        last_kernel,
        grid=(2 * steps,),
        in_specs=[
            first(2 * DH), first(2 * DH), second(2 * DH), second(2 * DH),
            pl.BlockSpec((1,) + w.shape[1:], lambda i: (0, 0, 0)),
            pl.BlockSpec((1, CHUNK, DH), lambda i: (1, late(i), 0)),
            pl.BlockSpec((1, CHUNK, DH), lambda i: (1, early(i), 0)),
            first(DH), second(DH),
        ],
        out_specs=pl.BlockSpec((CHUNK, DH), lambda i: (i, 0)),
        out_shape=shape(2 * rows, DH),
        compiler_params=params(24),
        cost_estimate=cost(2 * rows * 4 * DH * DH, 8 << 20),
        name="token_last",
    )(*a, *b, w, right1, left1, right2, left2)


def weights_kernel(after, y_ref, obs_ref, a_ref, b_ref, o0, o1, o2, o3, acc, blocks):
    step = pl.program_id(0)
    joined = jnp.where(step < pl.num_programs(0) // 2, a_ref[...], b_ref[...])
    j_hi, j_lo = split(joined)
    o_hi, o_lo = split(obs_ref[...])
    value = mm(j_hi, o_hi, 0, 0) + mm(j_lo, o_hi, 0, 0) + mm(j_hi, o_lo, 0, 0)

    @pl.when(step == 0)
    def _():
        acc[...] = value

    @pl.when(step > 0)
    def _():
        acc[...] += value

    @pl.when(step == pl.num_programs(0) - 1)
    def _():
        nz, own = o0.shape[0], o0.shape[1]
        for i in range(nz):
            group = acc[:, i * NY * own : (i + 1) * NY * own].T
            blocks[i] = group.reshape(NY, own, 2 * DH)
        for k, out in enumerate((o0, o1, o2, o3)):
            out[...] = blocks[:, lax.rem(y_ref[0] + k, NY)]


def weight_grads(dep, y, nz, observations, a, b):
    tok, width = observations.shape
    own = width // nz // NY
    steps = a.shape[0] // CHUNK
    return pl.pallas_call(
        weights_kernel,
        grid=(2 * steps,),
        in_specs=[
            ANY, SCALARS,
            pl.BlockSpec((CHUNK, width), lambda i: (i, 0)),
            pl.BlockSpec((CHUNK, 2 * DH), lambda i: (jnp.minimum(i, steps - 1), 0)),
            pl.BlockSpec((CHUNK, 2 * DH), lambda i: (jnp.maximum(i - steps, 0), 0)),
        ],
        out_specs=[pl.BlockSpec((nz, own, 2 * DH), lambda i: (0, 0, 0))] * NY,
        out_shape=[shape(nz, own, 2 * DH)] * NY,
        scratch_shapes=[VMEM((2 * DH, width), F32), VMEM((nz, NY, own, 2 * DH), F32)],
        compiler_params=params(24),
        cost_estimate=cost(tok * width * 2 * DH, 11 << 20),
        name="weight_grads",
    )(dep, y, observations, a, b)


def small_call(kernel, outs, operands, scalars, after=(), scratch=(), name=None):
    def body(*refs):
        kernel(*refs[len(after) :])

    return pl.pallas_call(
        body,
        in_specs=[ANY] * len(after) + [SCALARS] * len(scalars) + [WHOLE] * len(operands),
        out_specs=[WHOLE] * len(outs),
        out_shape=list(outs),
        scratch_shapes=list(scratch),
        compiler_params=params(24),
        cost_estimate=cost(1 << 20, 1 << 20),
        name=name,
    )(*after, *scalars, *operands)


def chip_weights_kernel(place_ref, wk_ref, wv_ref, taken_ref, out_ref):
    x, core = place_ref[0], place_ref[1]
    nx = out_ref.shape[0]
    for r in range(nx):
        d = lax.rem(x + r, nx)
        at = pl.ds(pl.multiple_of((2 * d + core) * DH, DH), DH)
        pieces = (wk_ref[at], wv_ref[at], taken_ref[d, :, :DH], taken_ref[d, :, DH:])
        for i, piece in enumerate(pieces):
            hi, lo = split(piece)
            cols = slice(i * DH, (i + 1) * DH)
            out_ref[r, :DH, cols], out_ref[r, DH:, cols] = hi, lo


def combine_kernel(stats_ref, stat_ref, shares_ref, deltas_ref):
    tops = stats_ref[:, 0, :]
    top = jnp.max(tops, axis=0, keepdims=True)
    weight = jnp.exp(tops - top)
    sums, mixes = stats_ref[:, 1, :], stats_ref[:, 2, :]
    total = jnp.sum(weight * sums, axis=0, keepdims=True)
    delta = jnp.sum(weight * mixes, axis=0, keepdims=True) / total
    stat_ref[0:1], stat_ref[1:2], stat_ref[2:3] = top, 1.0 / total, delta
    shares_ref[...] = (weight / total)[:, None]
    deltas_ref[...] = (mixes / sums - delta)[:, None]


def rows_kernel(scale, place_ref, shares_ref, deltas_ref, p0, p1, p2, p3, out_ref):
    z, y = place_ref[0], place_ref[1]
    rows = out_ref.shape[0]
    lanes = pl.ds(pl.multiple_of(y * rows, rows), rows)
    dq, att = 0.0, 0.0
    for k, part in enumerate((p0, p1, p2, p3)):
        source = z * NY + lax.rem(y + NY - k, NY)
        share = jnp.broadcast_to(shares_ref[source, :, lanes], (DH, rows)).T
        delta = jnp.broadcast_to(deltas_ref[source, :, lanes], (DH, rows)).T
        dq += share * (part[:, :DH] + delta * part[:, DH : 2 * DH])
        att += share * part[:, 2 * DH :]
    out_ref[:, :DH] = dq * scale
    out_ref[:, DH:] = att


def latent_part_kernel(both_ref, wq_ref, rows_ref, part_ref):
    rows = jnp.sum(both_ref[...], axis=0)
    rows_ref[...] = rows
    part = dot3(rows[:, :DH], wq_ref[...], 1, 1)
    for h in range(part_ref.shape[0]):
        part_ref[h] = part[:, h * DH : (h + 1) * DH]


def latent_rows_kernel(rows_ref, part_ref, w0, w1, w2, w3, out_ref):
    d_lat = jnp.sum(part_ref[...], axis=0)
    half = out_ref.shape[1]
    for i in range(out_ref.shape[0]):
        out_ref[i, :, : 2 * DH] = rows_ref[...]
        out_ref[i, :, 2 * DH : 3 * DH] = d_lat
        weights = (w0[i] + w1[i]) + (w2[i] + w3[i])
        out_ref[i, :, 3 * DH : 5 * DH] = weights[:half]
        out_ref[i, :, 5 * DH :] = weights[half:]


def gathered_kernel(got_ref, rows_ref, key_ref, value_ref):
    half = got_ref.shape[1]
    total = got_ref[0, :, 3 * DH :]
    for i in range(1, got_ref.shape[0]):
        total += got_ref[i, :, 3 * DH :]
    for i in range(got_ref.shape[0]):
        rows_ref[i * half : (i + 1) * half] = got_ref[i, :, : 3 * DH]
    key_ref[:half], key_ref[half:] = total[:, :DH], total[:, 2 * DH : 3 * DH]
    value_ref[:half], value_ref[half:] = total[:, DH : 2 * DH], total[:, 3 * DH :]


def final_kernel(y_ref, own, r1, r2, r3, lat_ref, dout_ref, d_lat_ref, d_wq_ref, d_wo_ref, both):
    rows = own.shape[0]
    for k, part in enumerate((own, r1, r2, r3)):
        at = pl.ds(pl.multiple_of(lax.rem(y_ref[0] + NY - k, NY) * rows, rows), rows)
        both[at] = part[:, : 2 * DH]
        d_lat_ref[at] = part[:, 2 * DH :]
    d_wq_ref[...] = dot3(lat_ref[...], both[:, :DH], 0, 0)
    d_wo_ref[...] = dot3(both[:, DH:], dout_ref[...], 0, 0)


def on_device(latents, observations, w_query, w_key, w_value, w_out, d_out):
    scale = 1.0 / math.sqrt(DH)
    lat = latents.shape[0]
    width = observations.shape[1]
    n_ctx, n_head = lax.axis_size("ctx"), lax.axis_size("head")
    nz, nx = n_ctx // NY, n_head // 2
    ctx, head = lax.axis_index("ctx"), lax.axis_index("head")
    z, y = ctx // NY, ctx % NY
    x, core = head // 2, head % 2
    z_groups = [[a * NY + b for a in range(nz)] for b in range(NY)]
    swap = [(i, i ^ 1) for i in range(n_head)]
    right = [(i, (i + 2) % n_head) for i in range(n_head)]
    left = [(i, (i - 2) % n_head) for i in range(n_head)]
    rows_y = lat // NY
    rows_z = rows_y // nz

    def along_y(k):
        return [(i, i - i % NY + (i + k) % NY) for i in range(n_ctx)]

    kv, q3, g3, sent, stat, given = forward(
        n_ctx, core.reshape(1), latents, d_out, w_query, w_out, w_key, w_value, observations
    )
    stats = lax.all_to_all(sent, "ctx", 0, 0)
    taken = lax.ppermute(given, "head", swap)
    parts = local_sums(y.reshape(1), kv, q3, g3, stat)
    parts = [parts[0]] + [lax.ppermute(parts[k], "ctx", along_y(k)) for k in range(1, NY)]
    (w_chip,) = small_call(
        chip_weights_kernel, [shape(nx, 2 * DH, 4 * DH, dtype=BF16)],
        [w_key, w_value, taken], [jnp.stack([x, core])], after=[parts[0]], name="chip_weights",
    )
    stat, shares, deltas = small_call(
        combine_kernel,
        [shape(3, lat), shape(n_ctx, 1, lat), shape(n_ctx, 1, lat)],
        [stats], [], after=[w_chip], name="combine",
    )

    def half_grads(h):
        own = token_grads(h, kv, q3, g3, stat)
        return own, lax.ppermute(own, "head", swap)

    a, b = half_grads(0), half_grads(1)
    half = a[0].shape[0]
    right_1, left_1 = token_part(
        first_kernel, a, b, w_chip, (2, 1, 3), b[0], (), [shape(2, half, DH)] * 2, "token_first"
    )
    from_left_1 = lax.ppermute(right_1, "head", right)
    from_right_1 = lax.ppermute(left_1, "head", left)

    (both,) = small_call(
        lambda *refs: rows_kernel(scale, *refs), [shape(rows_y, 2 * DH)],
        [shares, deltas, *parts], [jnp.stack([z, y])], after=[right_1], name="rows",
    )
    rows = lax.all_to_all(
        both.reshape(nz, rows_z, 2 * DH), "ctx", 0, 0, axis_index_groups=z_groups
    )
    d_w = weight_grads(both, y.reshape(1), nz, observations, a[0], b[0])
    d_w = [d_w[0]] + [lax.ppermute(d_w[k], "ctx", along_y(k)) for k in range(1, NY)]
    rows, part = small_call(
        latent_part_kernel, [shape(rows_z, 2 * DH), shape(n_head, rows_z, DH)],
        [rows, w_query], [], after=[d_w[0]], name="latent_part",
    )
    part = lax.all_to_all(part, "head", 0, 0)
    (sent,) = small_call(
        latent_rows_kernel, [shape(nz, rows_z, 7 * DH)], [rows, part, *d_w], [],
        name="latent_rows",
    )
    got = lax.all_to_all(sent, "ctx", 0, 0, axis_index_groups=z_groups)
    right_2, left_2 = token_part(
        second_kernel, a, b, w_chip, (1, 3), sent, (from_left_1, from_right_1),
        [shape(half, DH)] * 2, "token_second",
    )
    from_left_2 = lax.ppermute(right_2, "head", right)
    from_right_2 = lax.ppermute(left_2, "head", left)
    rows, d_w_key, d_w_value = small_call(
        gathered_kernel,
        [shape(rows_y, 3 * DH), shape(width // n_ctx, DH), shape(width // n_ctx, DH)],
        [got], [], after=[right_2], name="gathered",
    )
    rows = [rows] + [lax.ppermute(rows, "ctx", along_y(k)) for k in range(1, NY)]
    d_latents, d_w_query, d_w_out = small_call(
        final_kernel, [shape(lat, DH), shape(width, DH), shape(DH, width)],
        [*rows, latents, d_out], [y.reshape(1)], scratch=[VMEM((lat, 2 * DH), F32)], name="final",
    )
    d_observations = token_last(a, b, w_chip, from_left_1, from_right_1, from_left_2, from_right_2)
    return (d_latents, d_observations, d_w_query, d_w_key, d_w_value, d_w_out)


def solution(mesh):
    placed = (
        P(),
        P("ctx", None),
        P(None, "head"),
        P(None, "head"),
        P(None, "head"),
        P("head", None),
        P(),
    )
    return jax.shard_map(
        on_device,
        mesh=mesh,
        in_specs=placed,
        out_specs=(
            P(None, "head"),
            P("ctx", "head"),
            P(None, "head"),
            P("ctx", "head"),
            P("ctx", "head"),
            P("head", None),
        ),
        check_vma=False,
    )
```

```python
import math

import jax
import jax.numpy as jnp
from jax import lax
from jax.experimental import pallas as pl
from jax.experimental.pallas import tpu as pltpu
from jax.sharding import PartitionSpec as P

DH = 128
NY = 4
CHUNK = 512
F32 = jnp.float32
BF16 = jnp.bfloat16
VMEM = pltpu.VMEM
WHOLE = pl.BlockSpec(memory_space=VMEM)
ANY = pl.BlockSpec(memory_space=pl.ANY)
HBM = pl.BlockSpec(memory_space=pltpu.HBM)
SCALARS = pl.BlockSpec(memory_space=pltpu.SMEM)


def shape(*dims, dtype=F32):
    return jax.ShapeDtypeStruct(dims, dtype)


def pin(a, space):
    return pltpu.with_memory_space_constraint(a, space)


def params(mib):
    return pltpu.CompilerParams(vmem_limit_bytes=mib << 20)


def cost(macs, bytes_accessed):
    return pl.CostEstimate(flops=6 * macs, bytes_accessed=bytes_accessed, transcendentals=0)


def mm(a, b, ca=1, cb=0):
    return lax.dot_general(a, b, (((ca,), (cb,)), ((), ())), preferred_element_type=F32)


def split(a):
    hi = a.astype(BF16)
    return hi, (a - hi.astype(F32)).astype(BF16)


def dot3(a, b, ca=1, cb=0):
    a_hi, a_lo = split(a)
    b_hi, b_lo = split(b)
    return mm(a_hi, b_hi, ca, cb) + mm(a_hi, b_lo, ca, cb) + mm(a_lo, b_hi, ca, cb)


def scores_of(kv_ref, q3, g3):
    hi_k, hi_v, lo_k, lo_v = (kv_ref[:, i * DH : (i + 1) * DH] for i in range(4))
    scores = mm(jnp.concatenate([hi_k, lo_k, hi_k], axis=1), q3[...], 1, 1)
    return scores, mm(jnp.concatenate([hi_v, lo_v, hi_v], axis=1), g3[...], 1, 1)


def forward_kernel(
    scale, core_ref, lat_hbm, dout_hbm, wq_hbm, wo_hbm, wk_hbm, wv_hbm, obs_hbm,
    kv_ref, q3, g3, sent_ref, stat_ref, given_ref,
    lat_v, dout_v, wq_v, wo_v, wk_v, wv_v, obs_v, sems, obs_sems, w_hi, w_lo,
):
    step = pl.program_id(0)
    loads = [
        pltpu.make_async_copy(source, target, sems.at[i])
        for i, (source, target) in enumerate(
            (
                (wk_hbm, wk_v), (wv_hbm, wv_v), (lat_hbm, lat_v),
                (wq_hbm, wq_v), (dout_hbm, dout_v), (wo_hbm, wo_v),
            )
        )
    ]

    def load_tokens(i):
        rows = pl.ds(pl.multiple_of(i * CHUNK, CHUNK), CHUNK)
        return pltpu.make_async_copy(obs_hbm.at[rows], obs_v.at[i], obs_sems.at[i])

    @pl.when(step == 0)
    def _():
        loads[0].start()
        loads[1].start()
        load_tokens(0).start()
        for load in loads[2:]:
            load.start()
        for i in range(1, obs_v.shape[0]):
            load_tokens(i).start()
        loads[0].wait()
        loads[1].wait()
        hi, lo = split(wk_v[...])
        w_hi[:, :DH], w_lo[:, :DH] = hi, lo
        hi, lo = split(wv_v[...])
        w_hi[:, DH:], w_lo[:, DH:] = hi, lo
        for d in range(given_ref.shape[0]):
            at = pl.ds(pl.multiple_of((2 * d + 1 - core_ref[0]) * DH, DH), DH)
            given_ref[d, :, :DH], given_ref[d, :, DH:] = wk_v[at], wv_v[at]

    load_tokens(step).wait()
    o_hi, o_lo = split(obs_v[step])
    kv = mm(o_hi, w_hi[...]) + mm(o_hi, w_lo[...]) + mm(o_lo, w_hi[...])
    hi, lo = split(kv)
    kv_ref[:, : 2 * DH], kv_ref[:, 2 * DH :] = hi, lo

    @pl.when(step == 0)
    def _():
        loads[2].wait()
        loads[3].wait()
        top, bottom = split(dot3(lat_v[...], wq_v[...]) * scale)
        q3[:, :DH], q3[:, DH : 2 * DH], q3[:, 2 * DH :] = top, top, bottom
        loads[4].wait()
        loads[5].wait()
        top, bottom = split(dot3(dout_v[...], wo_v[...], 1, 1))
        g3[:, :DH], g3[:, DH : 2 * DH], g3[:, 2 * DH :] = top, top, bottom

    scores, dprobs = scores_of(kv_ref, q3, g3)
    top = jnp.max(scores, axis=0, keepdims=True)
    expo = jnp.exp(scores - top)
    total = jnp.sum(expo, axis=0, keepdims=True)
    mix = jnp.sum(expo * dprobs, axis=0, keepdims=True)

    @pl.when(step == 0)
    def _():
        stat_ref[0:1], stat_ref[1:2], stat_ref[2:3] = top, total, mix

    @pl.when(step > 0)
    def _():
        before = stat_ref[0:1]
        now = jnp.maximum(before, top)
        w_before, w_new = jnp.exp(before - now), jnp.exp(top - now)
        stat_ref[0:1] = now
        stat_ref[1:2] = stat_ref[1:2] * w_before + total * w_new
        stat_ref[2:3] = stat_ref[2:3] * w_before + mix * w_new

    @pl.when(step == pl.num_programs(0) - 1)
    def _():
        sent_ref[...] = jnp.broadcast_to(stat_ref[...][None], sent_ref.shape)


def forward(n_ctx, core, *arrays):
    latents, d_out, w_query, w_out, w_key, w_value, observations = arrays
    lat, tok, width = latents.shape[0], observations.shape[0], observations.shape[1]
    steps = tok // CHUNK
    nx = width // DH // 2
    block = lambda cols: pl.BlockSpec((CHUNK, cols), lambda i: (i, 0))
    full = lambda *dims: pl.BlockSpec(dims, lambda i: (0,) * len(dims))
    return pl.pallas_call(
        lambda *refs: forward_kernel(1.0 / math.sqrt(DH), *refs),
        grid=(steps,),
        in_specs=[SCALARS] + [HBM] * 7,
        out_specs=[
            block(4 * DH), full(lat, 3 * DH), full(lat, 3 * DH),
            full(n_ctx, 3, lat), full(3, lat), full(nx, DH, 2 * DH),
        ],
        out_shape=[
            shape(tok, 4 * DH, dtype=BF16),
            shape(lat, 3 * DH, dtype=BF16), shape(lat, 3 * DH, dtype=BF16),
            shape(n_ctx, 3, lat), shape(3, lat), shape(nx, DH, 2 * DH),
        ],
        scratch_shapes=[
            VMEM(latents.shape, F32), VMEM(d_out.shape, F32), VMEM(w_query.shape, F32),
            VMEM(w_out.shape, F32), VMEM(w_key.shape, F32), VMEM(w_value.shape, F32),
            VMEM((steps, CHUNK, width), F32),
            pltpu.SemaphoreType.DMA((6,)), pltpu.SemaphoreType.DMA((steps,)),
            VMEM((width, 2 * DH), BF16), VMEM((width, 2 * DH), BF16),
        ],
        compiler_params=params(60),
        cost_estimate=cost(tok * width * 256 + 2 * tok * lat * DH, 18 << 20),
        name="forward",
    )(core, *[pin(a, pltpu.HBM) for a in arrays])


def grads_kernel(scale, mark_ref, stats_ref, kv_ref, q3, g3, out_ref, rows_ref, stat, acc):
    step = pl.program_id(0)

    @pl.when(step == 0)
    def _():
        tops = stats_ref[:, 0, :]
        top = jnp.max(tops, axis=0, keepdims=True)
        weight = jnp.exp(tops - top)
        total = jnp.sum(weight * stats_ref[:, 1, :], axis=0, keepdims=True)
        mix = jnp.sum(weight * stats_ref[:, 2, :], axis=0, keepdims=True)
        stat[0:1], stat[1:2], stat[2:3] = top, 1.0 / total, mix / total

    scores, dprobs = scores_of(kv_ref, q3, g3)
    probs = jnp.exp(scores - stat[0:1]) * stat[1:2]
    dscores = probs * (dprobs - stat[2:3])
    for at, value, packed in ((0, dscores, q3), (DH, probs, g3)):
        hi, lo = split(value)
        both = mm(hi, packed[:, DH:])
        out_ref[:, at : at + DH] = both[:, :DH] + both[:, DH:] + mm(lo, packed[:, :DH])
        t_hi, t_lo = kv_ref[:, at : at + DH], kv_ref[:, 2 * DH + at : 3 * DH + at]
        both = mm(jnp.concatenate([t_hi, t_lo], axis=1), hi, 0, 0)
        sums = both[:DH] + both[DH:] + mm(t_hi, lo, 0, 0)
        acc[at : at + DH] = jnp.where(step == 0, sums, acc[at : at + DH] + sums)

    @pl.when(step == pl.num_programs(0) - 1)
    def _():
        rows_ref[:, :DH] = acc[:DH].T * scale
        rows_ref[:, DH:] = acc[DH:].T


def token_grads(mark, stats, kv, q3, g3):
    tok, lat = kv.shape[0], q3.shape[0]
    return pl.pallas_call(
        lambda *refs: grads_kernel(1.0 / math.sqrt(DH), *refs),
        grid=(tok // CHUNK,),
        in_specs=[WHOLE, WHOLE, pl.BlockSpec((CHUNK, 4 * DH), lambda i: (i, 0)), WHOLE, WHOLE],
        out_specs=[
            pl.BlockSpec((CHUNK, 2 * DH), lambda i: (i, 0)),
            pl.BlockSpec((lat, 2 * DH), lambda i: (0, 0)),
        ],
        out_shape=[shape(tok, 2 * DH), shape(lat, 2 * DH)],
        scratch_shapes=[VMEM((3, lat), F32), VMEM((2 * DH, lat), F32)],
        compiler_params=params(60),
        cost_estimate=cost(6 * tok * lat * DH, 6 << 20),
        name="token_grads",
    )(mark, stats, kv, q3, g3)


def project(own, other, w):
    o_hi, o_lo = split(own)
    t_hi, t_lo = split(other)
    hi = jnp.concatenate([o_hi, t_hi], axis=1)
    lo = jnp.concatenate([o_lo, t_lo], axis=1)
    both = mm(hi, w, 1, 1)
    return both[:, :DH] + both[:, DH:] + mm(lo, w[:DH], 1, 1)


def first_kernel(own_a, other_a, own_b, other_b, far, near, back, right_ref, left_ref):
    a, b = (own_a[...], other_a[...]), (own_b[...], other_b[...])
    right_ref[0] = project(*a, far[0])
    right_ref[1] = project(*b, near[0])
    left_ref[0] = project(*b, far[0])
    left_ref[1] = project(*a, back[0])


def rest_kernel(own_a, other_a, own_b, other_b, home, near, back, right_ref, left_ref, out_ref):
    a, b = (own_a[...], other_a[...]), (own_b[...], other_b[...])
    right_ref[...] = project(*a, near[0])
    left_ref[...] = project(*b, back[0])
    out_ref[0] = project(*a, home[0])
    out_ref[1] = project(*b, home[0])


def token_part(kernel, own, other, w, which, outs, name, mib):
    half = own.shape[0] // 2
    steps = half // CHUNK
    a = pl.BlockSpec((CHUNK, 2 * DH), lambda i: (i, 0))
    b = pl.BlockSpec((CHUNK, 2 * DH), lambda i: (i + steps, 0))
    pair = pl.BlockSpec((2, CHUNK, DH), lambda i: (0, i, 0))
    one = pl.BlockSpec((CHUNK, DH), lambda i: (i, 0))
    chosen = [pl.BlockSpec((1,) + w.shape[1:], lambda i, k=k: (k, 0, 0)) for k in which]
    return pl.pallas_call(
        kernel,
        grid=(steps,),
        in_specs=[a, a, b, b] + chosen,
        out_specs=[pair if len(o.shape) == 3 else one for o in outs],
        out_shape=outs,
        compiler_params=params(mib),
        cost_estimate=cost(4 * half * 4 * DH * DH, 6 << 20),
        name=name,
    )(own, other, own, other, *[w] * len(which))


def weights_kernel(y_ref, obs_ref, joined_ref, o0, o1, o2, o3, acc, blocks):
    step = pl.program_id(0)
    joined = joined_ref[...]
    j_hi, j_lo = split(joined)
    o_hi, o_lo = split(obs_ref[...])
    value = mm(j_hi, o_hi, 0, 0) + mm(j_lo, o_hi, 0, 0) + mm(j_hi, o_lo, 0, 0)

    @pl.when(step == 0)
    def _():
        acc[...] = value

    @pl.when(step > 0)
    def _():
        acc[...] += value

    @pl.when(step == pl.num_programs(0) - 1)
    def _():
        nz, own = o0.shape[0], o0.shape[1]
        for i in range(nz):
            group = acc[:, i * NY * own : (i + 1) * NY * own].T
            blocks[i] = group.reshape(NY, own, 2 * DH)
        for k, out in enumerate((o0, o1, o2, o3)):
            out[...] = blocks[:, lax.rem(y_ref[0] + k, NY)]


def weight_grads(y, nz, observations, joined):
    tok, width = observations.shape
    own = width // nz // NY
    return pl.pallas_call(
        weights_kernel,
        grid=(tok // CHUNK,),
        in_specs=[
            SCALARS,
            pl.BlockSpec((CHUNK, width), lambda i: (i, 0)),
            pl.BlockSpec((CHUNK, 2 * DH), lambda i: (i, 0)),
        ],
        out_specs=[pl.BlockSpec((nz, own, 2 * DH), lambda i: (0, 0, 0))] * NY,
        out_shape=[shape(nz, own, 2 * DH)] * NY,
        scratch_shapes=[VMEM((2 * DH, width), F32), VMEM((nz, NY, own, 2 * DH), F32)],
        compiler_params=params(60),
        cost_estimate=cost(tok * width * 2 * DH, 11 << 20),
        name="weight_grads",
    )(y, observations, joined)


def small_call(kernel, outs, operands, scalars, after=(), scratch=(), name=None):
    def body(*refs):
        kernel(*refs[len(after) :])

    return pl.pallas_call(
        body,
        in_specs=[ANY] * len(after) + [SCALARS] * len(scalars) + [WHOLE] * len(operands),
        out_specs=[WHOLE] * len(outs),
        out_shape=list(outs),
        scratch_shapes=list(scratch),
        compiler_params=params(24),
        cost_estimate=cost(1 << 20, 1 << 20),
        name=name,
    )(*after, *scalars, *operands)


def loaded_call(kernel, outs, operands, scalars, after=(), mib=24, name=None):
    n_skip, n_scalars, n = len(after), len(scalars), len(operands)

    def body(*refs):
        refs = refs[n_skip:]
        sources, others = refs[n_scalars : n_scalars + n], refs[n_scalars + n :]
        results, buffers, sems = others[: len(outs)], others[len(outs) : -1], others[-1]
        loads = [
            pltpu.make_async_copy(source, buffer, sems.at[i])
            for i, (source, buffer) in enumerate(zip(sources, buffers))
        ]
        for load in loads:
            load.start()
        for load in loads:
            load.wait()
        kernel(*refs[:n_scalars], *buffers, *results)

    return pl.pallas_call(
        body,
        in_specs=[ANY] * n_skip + [SCALARS] * n_scalars + [ANY] * n,
        out_specs=[WHOLE] * len(outs),
        out_shape=list(outs),
        scratch_shapes=[VMEM(a.shape, a.dtype) for a in operands]
        + [pltpu.SemaphoreType.DMA((n,))],
        compiler_params=params(mib),
        cost_estimate=cost(1 << 20, 1 << 20),
        name=name,
    )(*after, *scalars, *operands)


def chip_weights_kernel(place_ref, wk_ref, wv_ref, taken_ref, out_ref, mark_ref):
    x, core = place_ref[0], place_ref[1]
    mark_ref[...] = jnp.zeros_like(mark_ref)
    nx = out_ref.shape[0]
    for r in range(nx):
        d = lax.rem(x + r, nx)
        at = pl.ds(pl.multiple_of((2 * d + core) * DH, DH), DH)
        pieces = (wk_ref[at], wv_ref[at], taken_ref[d, :, :DH], taken_ref[d, :, DH:])
        for i, piece in enumerate(pieces):
            hi, lo = split(piece)
            cols = slice(i * DH, (i + 1) * DH)
            out_ref[r, :DH, cols], out_ref[r, DH:, cols] = hi, lo


def second_kernel(near, back, from_left, from_right, right_ref, left_ref):
    right_ref[...] = near[...] + from_left[0]
    left_ref[...] = back[...] + from_right[0]


def last_kernel(home, left1, right1, left2, right2, out_ref, mark_ref):
    mark_ref[...] = jnp.zeros_like(mark_ref)
    half = home.shape[1]
    out_ref[:half] = home[0] + left2[...] + right1[1]
    out_ref[half:] = home[1] + left1[1] + right2[...]


def latent_part_kernel(both_ref, wq_ref, rows_ref, part_ref):
    rows = jnp.sum(both_ref[...], axis=0)
    rows_ref[...] = rows
    part = dot3(rows[:, :DH], wq_ref[...], 1, 1)
    for h in range(part_ref.shape[0]):
        part_ref[h] = part[:, h * DH : (h + 1) * DH]


def latent_rows_kernel(rows_ref, part_ref, w0, w1, w2, w3, out_ref):
    d_lat = jnp.sum(part_ref[...], axis=0)
    half = out_ref.shape[1]
    for i in range(out_ref.shape[0]):
        out_ref[i, :, : 2 * DH] = rows_ref[...]
        out_ref[i, :, 2 * DH : 3 * DH] = d_lat
        weights = (w0[i] + w1[i]) + (w2[i] + w3[i])
        out_ref[i, :, 3 * DH : 5 * DH] = weights[:half]
        out_ref[i, :, 5 * DH :] = weights[half:]


def gathered_kernel(got_ref, rows_ref, key_ref, value_ref):
    half = got_ref.shape[1]
    total = got_ref[0, :, 3 * DH :]
    for i in range(1, got_ref.shape[0]):
        total += got_ref[i, :, 3 * DH :]
    for i in range(got_ref.shape[0]):
        rows_ref[i * half : (i + 1) * half] = got_ref[i, :, : 3 * DH]
    key_ref[:half], key_ref[half:] = total[:, :DH], total[:, 2 * DH : 3 * DH]
    value_ref[:half], value_ref[half:] = total[:, DH : 2 * DH], total[:, 3 * DH :]


def final_kernel(y_ref, _, own, r1, r2, r3, lat_ref, dout_ref, d_lat_ref, d_wq_ref, d_wo_ref, all_rows):
    nz, rows = all_rows.shape[0], all_rows.shape[2]
    for k, part in enumerate((own, r1, r2, r3)):
        all_rows[:, lax.rem(y_ref[0] + NY - k, NY)] = part[...].reshape(nz, rows, 3 * DH)
    both = all_rows[...].reshape(d_lat_ref.shape[0], 3 * DH)
    d_lat_ref[...] = both[:, 2 * DH :]
    d_wq_ref[...] = dot3(lat_ref[...], both[:, :DH], 0, 0)
    d_wo_ref[...] = dot3(both[:, DH : 2 * DH], dout_ref[...], 0, 0)


def on_device(latents, observations, w_query, w_key, w_value, w_out, d_out):
    lat = latents.shape[0]
    width = observations.shape[1]
    n_ctx, n_head = lax.axis_size("ctx"), lax.axis_size("head")
    nz, nx = n_ctx // NY, n_head // 2
    ctx, head = lax.axis_index("ctx"), lax.axis_index("head")
    z, y = ctx // NY, ctx % NY
    x, core = head // 2, head % 2
    z_groups = [[a * NY + b for a in range(nz)] for b in range(NY)]
    swap = [(i, i ^ 1) for i in range(n_head)]
    right = [(i, (i + 2) % n_head) for i in range(n_head)]
    left = [(i, (i - 2) % n_head) for i in range(n_head)]
    rows_z = lat // n_ctx
    rows_y = rows_z * nz

    def along_y(k):
        return [(i, i - i % NY + (i + k) % NY) for i in range(n_ctx)]

    kv, q3, g3, sent, stat, given = forward(
        n_ctx, core.reshape(1), latents, d_out, w_query, w_out, w_key, w_value, observations
    )
    stats = lax.all_to_all(sent, "ctx", 0, 0)
    taken = lax.ppermute(given, "head", swap)
    w_chip, mark = small_call(
        chip_weights_kernel, [shape(nx, 2 * DH, 4 * DH, dtype=BF16), shape(8, DH)],
        [w_key, w_value, taken], [jnp.stack([x, core])], name="chip_weights",
    )
    own, rows = token_grads(mark, stats, kv, q3, g3)

    half = own.shape[0] // 2
    other = lax.ppermute(own, "head", swap)
    rows = lax.all_to_all(rows.reshape(n_ctx, rows_z, 2 * DH), "ctx", 0, 0)
    d_w = weight_grads(y.reshape(1), nz, observations, own)
    d_w = [d_w[0]] + [lax.ppermute(d_w[k], "ctx", along_y(k)) for k in range(1, NY)]
    right_1, left_1 = token_part(
        first_kernel, own, other, w_chip, (2, 1, 3), [shape(2, half, DH)] * 2, "token_first", 60
    )
    from_left_1 = lax.ppermute(right_1, "head", right)
    from_right_1 = lax.ppermute(left_1, "head", left)
    near, back, home = token_part(
        rest_kernel, own, other, w_chip, (0, 1, 3),
        [shape(half, DH), shape(half, DH), shape(2, half, DH)], "token_rest", 24,
    )

    rows, part = loaded_call(
        latent_part_kernel, [shape(rows_z, 2 * DH), shape(n_head, rows_z, DH)],
        [rows, w_query], [], name="latent_part",
    )
    part = lax.all_to_all(part, "head", 0, 0)
    (sent,) = small_call(
        latent_rows_kernel, [shape(nz, rows_z, 7 * DH)], [rows, part, *d_w], [],
        name="latent_rows",
    )
    got = lax.all_to_all(sent, "ctx", 0, 0, axis_index_groups=z_groups)
    right_2, left_2 = small_call(
        second_kernel, [shape(half, DH)] * 2, [near, back, from_left_1, from_right_1], [],
        name="token_second",
    )
    from_left_2 = lax.ppermute(right_2, "head", right)
    from_right_2 = lax.ppermute(left_2, "head", left)
    rows, d_w_key, d_w_value = small_call(
        gathered_kernel,
        [shape(rows_y, 3 * DH), shape(width // n_ctx, DH), shape(width // n_ctx, DH)],
        [got], [], name="gathered",
    )
    rows = [rows] + [lax.ppermute(rows, "ctx", along_y(k)) for k in range(1, NY)]
    d_observations, mark = small_call(
        last_kernel, [shape(2 * half, DH), shape(8, DH)],
        [home, from_left_1, from_right_1, from_left_2, from_right_2], [], name="token_last",
    )
    d_latents, d_w_query, d_w_out = small_call(
        final_kernel, [shape(lat, DH), shape(width, DH), shape(DH, width)],
        [mark, *rows, latents, d_out], [y.reshape(1)],
        scratch=[VMEM((nz, NY, rows_z, 3 * DH), F32)], name="final",
    )
    return (d_latents, d_observations, d_w_query, d_w_key, d_w_value, d_w_out)


def solution(mesh):
    placed = (
        P(),
        P("ctx", None),
        P(None, "head"),
        P(None, "head"),
        P(None, "head"),
        P("head", None),
        P(),
    )
    return jax.shard_map(
        on_device,
        mesh=mesh,
        in_specs=placed,
        out_specs=(
            P(None, "head"),
            P("ctx", "head"),
            P(None, "head"),
            P("ctx", "head"),
            P("ctx", "head"),
            P("head", None),
        ),
        check_vma=False,
    )
```

```python
import math

import jax
import jax.numpy as jnp
from jax import lax
from jax.experimental import pallas as pl
from jax.experimental.pallas import tpu as pltpu
from jax.sharding import PartitionSpec as P

DH = 128
NY = 4
CHUNK = 512
F32 = jnp.float32
BF16 = jnp.bfloat16
VMEM = pltpu.VMEM
WHOLE = pl.BlockSpec(memory_space=VMEM)
ANY = pl.BlockSpec(memory_space=pl.ANY)
HBM = pl.BlockSpec(memory_space=pltpu.HBM)
SCALARS = pl.BlockSpec(memory_space=pltpu.SMEM)


def shape(*dims, dtype=F32):
    return jax.ShapeDtypeStruct(dims, dtype)


def pin(a, space):
    return pltpu.with_memory_space_constraint(a, space)


def params(mib):
    return pltpu.CompilerParams(vmem_limit_bytes=mib << 20)


def cost(macs, bytes_accessed):
    return pl.CostEstimate(flops=6 * macs, bytes_accessed=bytes_accessed, transcendentals=0)


def mm(a, b, ca=1, cb=0):
    return lax.dot_general(a, b, (((ca,), (cb,)), ((), ())), preferred_element_type=F32)


def split(a):
    hi = a.astype(BF16)
    return hi, (a - hi.astype(F32)).astype(BF16)


def dot3(a, b, ca=1, cb=0):
    a_hi, a_lo = split(a)
    b_hi, b_lo = split(b)
    return mm(a_hi, b_hi, ca, cb) + mm(a_hi, b_lo, ca, cb) + mm(a_lo, b_hi, ca, cb)


def scores_of(kv_ref, q3, g3):
    hi_k, hi_v, lo_k, lo_v = (kv_ref[:, i * DH : (i + 1) * DH] for i in range(4))
    scores = mm(jnp.concatenate([hi_k, lo_k, hi_k], axis=1), q3[...], 1, 1)
    return scores, mm(jnp.concatenate([hi_v, lo_v, hi_v], axis=1), g3[...], 1, 1)


def forward_kernel(
    scale, core_ref, lat_hbm, dout_hbm, wq_hbm, wo_hbm, wk_hbm, wv_hbm, obs_hbm,
    kv_ref, q3, g3, sent_ref, stat_ref, given_ref,
    lat_v, dout_v, wq_v, wo_v, wk_v, wv_v, obs_v, sems, obs_sems, w_hi, w_lo,
):
    step = pl.program_id(0)
    loads = [
        pltpu.make_async_copy(source, target, sems.at[i])
        for i, (source, target) in enumerate(
            (
                (wk_hbm, wk_v), (wv_hbm, wv_v), (lat_hbm, lat_v),
                (wq_hbm, wq_v), (dout_hbm, dout_v), (wo_hbm, wo_v),
            )
        )
    ]

    def load_tokens(i):
        rows = pl.ds(pl.multiple_of(i * CHUNK, CHUNK), CHUNK)
        return pltpu.make_async_copy(obs_hbm.at[rows], obs_v.at[i], obs_sems.at[i])

    @pl.when(step == 0)
    def _():
        loads[0].start()
        loads[1].start()
        load_tokens(0).start()
        for load in loads[2:]:
            load.start()
        for i in range(1, obs_v.shape[0]):
            load_tokens(i).start()
        loads[0].wait()
        loads[1].wait()
        hi, lo = split(wk_v[...])
        w_hi[:, :DH], w_lo[:, :DH] = hi, lo
        hi, lo = split(wv_v[...])
        w_hi[:, DH:], w_lo[:, DH:] = hi, lo
        for d in range(given_ref.shape[0]):
            at = pl.ds(pl.multiple_of((2 * d + 1 - core_ref[0]) * DH, DH), DH)
            given_ref[d, :, :DH], given_ref[d, :, DH:] = wk_v[at], wv_v[at]

    load_tokens(step).wait()
    o_hi, o_lo = split(obs_v[step])
    kv = mm(o_hi, w_hi[...]) + mm(o_hi, w_lo[...]) + mm(o_lo, w_hi[...])
    hi, lo = split(kv)
    kv_ref[:, : 2 * DH], kv_ref[:, 2 * DH :] = hi, lo

    @pl.when(step == 0)
    def _():
        loads[2].wait()
        loads[3].wait()
        top, bottom = split(dot3(lat_v[...], wq_v[...]) * scale)
        q3[:, :DH], q3[:, DH : 2 * DH], q3[:, 2 * DH :] = top, top, bottom
        loads[4].wait()
        loads[5].wait()
        top, bottom = split(dot3(dout_v[...], wo_v[...], 1, 1))
        g3[:, :DH], g3[:, DH : 2 * DH], g3[:, 2 * DH :] = top, top, bottom

    scores, dprobs = scores_of(kv_ref, q3, g3)
    top = jnp.max(scores, axis=0, keepdims=True)
    expo = jnp.exp(scores - top)
    total = jnp.sum(expo, axis=0, keepdims=True)
    mix = jnp.sum(expo * dprobs, axis=0, keepdims=True)

    @pl.when(step == 0)
    def _():
        stat_ref[0:1], stat_ref[1:2], stat_ref[2:3] = top, total, mix

    @pl.when(step > 0)
    def _():
        before = stat_ref[0:1]
        now = jnp.maximum(before, top)
        w_before, w_new = jnp.exp(before - now), jnp.exp(top - now)
        stat_ref[0:1] = now
        stat_ref[1:2] = stat_ref[1:2] * w_before + total * w_new
        stat_ref[2:3] = stat_ref[2:3] * w_before + mix * w_new

    @pl.when(step == pl.num_programs(0) - 1)
    def _():
        sent_ref[...] = jnp.broadcast_to(stat_ref[...][None], sent_ref.shape)


def forward(n_ctx, core, *arrays):
    latents, d_out, w_query, w_out, w_key, w_value, observations = arrays
    lat, tok, width = latents.shape[0], observations.shape[0], observations.shape[1]
    steps = tok // CHUNK
    nx = width // DH // 2
    block = lambda cols: pl.BlockSpec((CHUNK, cols), lambda i: (i, 0))
    full = lambda *dims: pl.BlockSpec(dims, lambda i: (0,) * len(dims))
    return pl.pallas_call(
        lambda *refs: forward_kernel(1.0 / math.sqrt(DH), *refs),
        grid=(steps,),
        in_specs=[SCALARS] + [HBM] * 7,
        out_specs=[
            block(4 * DH), full(lat, 3 * DH), full(lat, 3 * DH),
            full(n_ctx, 3, lat), full(3, lat), full(nx, DH, 2 * DH),
        ],
        out_shape=[
            shape(tok, 4 * DH, dtype=BF16),
            shape(lat, 3 * DH, dtype=BF16), shape(lat, 3 * DH, dtype=BF16),
            shape(n_ctx, 3, lat), shape(3, lat), shape(nx, DH, 2 * DH),
        ],
        scratch_shapes=[
            VMEM(latents.shape, F32), VMEM(d_out.shape, F32), VMEM(w_query.shape, F32),
            VMEM(w_out.shape, F32), VMEM(w_key.shape, F32), VMEM(w_value.shape, F32),
            VMEM((steps, CHUNK, width), F32),
            pltpu.SemaphoreType.DMA((6,)), pltpu.SemaphoreType.DMA((steps,)),
            VMEM((width, 2 * DH), BF16), VMEM((width, 2 * DH), BF16),
        ],
        compiler_params=params(60),
        cost_estimate=cost(tok * width * 256 + 2 * tok * lat * DH, 18 << 20),
        name="forward",
    )(core, *[pin(a, pltpu.HBM) for a in arrays])


def grads_kernel(scale, mark_ref, stats_ref, kv_ref, q3, g3, out_ref, rows_ref, stat, acc):
    step = pl.program_id(0)

    @pl.when(step == 0)
    def _():
        tops = stats_ref[:, 0, :]
        top = jnp.max(tops, axis=0, keepdims=True)
        weight = jnp.exp(tops - top)
        total = jnp.sum(weight * stats_ref[:, 1, :], axis=0, keepdims=True)
        mix = jnp.sum(weight * stats_ref[:, 2, :], axis=0, keepdims=True)
        stat[0:1], stat[1:2], stat[2:3] = top, 1.0 / total, mix / total

    scores, dprobs = scores_of(kv_ref, q3, g3)
    probs = jnp.exp(scores - stat[0:1]) * stat[1:2]
    dscores = probs * (dprobs - stat[2:3])
    for at, value, packed in ((0, dscores, q3), (DH, probs, g3)):
        hi, lo = split(value)
        both = mm(hi, packed[:, DH:])
        out_ref[:, at : at + DH] = both[:, :DH] + both[:, DH:] + mm(lo, packed[:, :DH])
        t_hi, t_lo = kv_ref[:, at : at + DH], kv_ref[:, 2 * DH + at : 3 * DH + at]
        both = mm(jnp.concatenate([t_hi, t_lo], axis=1), hi, 0, 0)
        sums = both[:DH] + both[DH:] + mm(t_hi, lo, 0, 0)
        acc[at : at + DH] = jnp.where(step == 0, sums, acc[at : at + DH] + sums)

    @pl.when(step == pl.num_programs(0) - 1)
    def _():
        rows_ref[:, :DH] = acc[:DH].T * scale
        rows_ref[:, DH:] = acc[DH:].T


def token_grads(mark, stats, kv, q3, g3):
    tok, lat = kv.shape[0], q3.shape[0]
    return pl.pallas_call(
        lambda *refs: grads_kernel(1.0 / math.sqrt(DH), *refs),
        grid=(tok // CHUNK,),
        in_specs=[WHOLE, WHOLE, pl.BlockSpec((CHUNK, 4 * DH), lambda i: (i, 0)), WHOLE, WHOLE],
        out_specs=[
            pl.BlockSpec((CHUNK, 2 * DH), lambda i: (i, 0)),
            pl.BlockSpec((lat, 2 * DH), lambda i: (0, 0)),
        ],
        out_shape=[shape(tok, 2 * DH), shape(lat, 2 * DH)],
        scratch_shapes=[VMEM((3, lat), F32), VMEM((2 * DH, lat), F32)],
        compiler_params=params(60),
        cost_estimate=cost(6 * tok * lat * DH, 6 << 20),
        name="token_grads",
    )(mark, stats, kv, q3, g3)


def project(own, other, w):
    o_hi, o_lo = split(own)
    t_hi, t_lo = split(other)
    hi = jnp.concatenate([o_hi, t_hi], axis=1)
    lo = jnp.concatenate([o_lo, t_lo], axis=1)
    both = mm(hi, w, 1, 1)
    return both[:, :DH] + both[:, DH:] + mm(lo, w[:DH], 1, 1)


def first_kernel(own_a, other_a, own_b, other_b, far, near, back, right_ref, left_ref):
    a, b = (own_a[...], other_a[...]), (own_b[...], other_b[...])
    right_ref[0] = project(*a, far[0])
    right_ref[1] = project(*b, near[0])
    left_ref[0] = project(*b, far[0])
    left_ref[1] = project(*a, back[0])


def rest_kernel(own_a, other_a, own_b, other_b, home, near, back, right_ref, left_ref, out_ref):
    a, b = (own_a[...], other_a[...]), (own_b[...], other_b[...])
    right_ref[...] = project(*a, near[0])
    left_ref[...] = project(*b, back[0])
    out_ref[0] = project(*a, home[0])
    out_ref[1] = project(*b, home[0])


def token_part(kernel, own, other, w, which, outs, name, mib):
    half = own.shape[0] // 2
    steps = half // CHUNK
    a = pl.BlockSpec((CHUNK, 2 * DH), lambda i: (i, 0))
    b = pl.BlockSpec((CHUNK, 2 * DH), lambda i: (i + steps, 0))
    pair = pl.BlockSpec((2, CHUNK, DH), lambda i: (0, i, 0))
    one = pl.BlockSpec((CHUNK, DH), lambda i: (i, 0))
    chosen = [pl.BlockSpec((1,) + w.shape[1:], lambda i, k=k: (k, 0, 0)) for k in which]
    return pl.pallas_call(
        kernel,
        grid=(steps,),
        in_specs=[a, a, b, b] + chosen,
        out_specs=[pair if len(o.shape) == 3 else one for o in outs],
        out_shape=outs,
        compiler_params=params(mib),
        cost_estimate=cost(4 * half * 4 * DH * DH, 6 << 20),
        name=name,
    )(own, other, own, other, *[w] * len(which))


def weights_kernel(y_ref, obs_hbm, joined_hbm, o0, o1, o2, o3, acc, blocks, obs_v, joined_v, sems):
    step = pl.program_id(0)

    def loads(i):
        rows = pl.ds(pl.multiple_of(i * CHUNK, CHUNK), CHUNK)
        return (
            pltpu.make_async_copy(obs_hbm.at[rows], obs_v.at[i], sems.at[0, i]),
            pltpu.make_async_copy(joined_hbm.at[rows], joined_v.at[i], sems.at[1, i]),
        )

    @pl.when(step == 0)
    def _():
        for i in range(obs_v.shape[0]):
            for load in loads(i):
                load.start()

    for load in loads(step):
        load.wait()
    joined = joined_v[step]
    j_hi, j_lo = split(joined)
    o_hi, o_lo = split(obs_v[step])
    value = mm(j_hi, o_hi, 0, 0) + mm(j_lo, o_hi, 0, 0) + mm(j_hi, o_lo, 0, 0)

    @pl.when(step == 0)
    def _():
        acc[...] = value

    @pl.when(step > 0)
    def _():
        acc[...] += value

    @pl.when(step == pl.num_programs(0) - 1)
    def _():
        nz, own = o0.shape[0], o0.shape[1]
        for i in range(nz):
            group = acc[:, i * NY * own : (i + 1) * NY * own].T
            blocks[i] = group.reshape(NY, own, 2 * DH)
        for k, out in enumerate((o0, o1, o2, o3)):
            out[...] = blocks[:, lax.rem(y_ref[0] + k, NY)]


def weight_grads(y, nz, observations, joined):
    tok, width = observations.shape
    own = width // nz // NY
    return pl.pallas_call(
        weights_kernel,
        grid=(tok // CHUNK,),
        in_specs=[
            SCALARS,
            HBM, HBM,
        ],
        out_specs=[pl.BlockSpec((nz, own, 2 * DH), lambda i: (0, 0, 0))] * NY,
        out_shape=[shape(nz, own, 2 * DH)] * NY,
        scratch_shapes=[
            VMEM((2 * DH, width), F32), VMEM((nz, NY, own, 2 * DH), F32),
            VMEM((tok // CHUNK, CHUNK, width), F32), VMEM((tok // CHUNK, CHUNK, 2 * DH), F32),
            pltpu.SemaphoreType.DMA((2, tok // CHUNK)),
        ],
        compiler_params=params(60),
        cost_estimate=cost(tok * width * 2 * DH, 11 << 20),
        name="weight_grads",
    )(y, observations, joined)


def small_call(kernel, outs, operands, scalars, after=(), scratch=(), name=None):
    def body(*refs):
        kernel(*refs[len(after) :])

    return pl.pallas_call(
        body,
        in_specs=[ANY] * len(after) + [SCALARS] * len(scalars) + [WHOLE] * len(operands),
        out_specs=[WHOLE] * len(outs),
        out_shape=list(outs),
        scratch_shapes=list(scratch),
        compiler_params=params(24),
        cost_estimate=cost(1 << 20, 1 << 20),
        name=name,
    )(*after, *scalars, *operands)


def loaded_call(kernel, outs, operands, scalars, after=(), mib=24, name=None):
    n_skip, n_scalars, n = len(after), len(scalars), len(operands)

    def body(*refs):
        refs = refs[n_skip:]
        sources, others = refs[n_scalars : n_scalars + n], refs[n_scalars + n :]
        results, buffers, sems = others[: len(outs)], others[len(outs) : -1], others[-1]
        loads = [
            pltpu.make_async_copy(source, buffer, sems.at[i])
            for i, (source, buffer) in enumerate(zip(sources, buffers))
        ]
        for load in loads:
            load.start()
        for load in loads:
            load.wait()
        kernel(*refs[:n_scalars], *buffers, *results)

    return pl.pallas_call(
        body,
        in_specs=[ANY] * n_skip + [SCALARS] * n_scalars + [ANY] * n,
        out_specs=[WHOLE] * len(outs),
        out_shape=list(outs),
        scratch_shapes=[VMEM(a.shape, a.dtype) for a in operands]
        + [pltpu.SemaphoreType.DMA((n,))],
        compiler_params=params(mib),
        cost_estimate=cost(1 << 20, 1 << 20),
        name=name,
    )(*after, *scalars, *operands)


def chip_weights_kernel(place_ref, wk_ref, wv_ref, taken_ref, out_ref, mark_ref):
    x, core = place_ref[0], place_ref[1]
    mark_ref[...] = jnp.zeros_like(mark_ref)
    nx = out_ref.shape[0]
    for r in range(nx):
        d = lax.rem(x + r, nx)
        at = pl.ds(pl.multiple_of((2 * d + core) * DH, DH), DH)
        pieces = (wk_ref[at], wv_ref[at], taken_ref[d, :, :DH], taken_ref[d, :, DH:])
        for i, piece in enumerate(pieces):
            hi, lo = split(piece)
            cols = slice(i * DH, (i + 1) * DH)
            out_ref[r, :DH, cols], out_ref[r, DH:, cols] = hi, lo


def second_kernel(near, back, from_left, from_right, right_ref, left_ref):
    right_ref[...] = near[...] + from_left[0]
    left_ref[...] = back[...] + from_right[0]


def last_kernel(home, left1, right1, left2, right2, out_ref, mark_ref):
    mark_ref[...] = jnp.zeros_like(mark_ref)
    half = home.shape[1]
    out_ref[:half] = home[0] + left2[...] + right1[1]
    out_ref[half:] = home[1] + left1[1] + right2[...]


def latent_part_kernel(both_ref, wq_ref, rows_ref, part_ref):
    rows = jnp.sum(both_ref[...], axis=0)
    rows_ref[...] = rows
    part = dot3(rows[:, :DH], wq_ref[...], 1, 1)
    for h in range(part_ref.shape[0]):
        part_ref[h] = part[:, h * DH : (h + 1) * DH]


def latent_rows_kernel(rows_ref, part_ref, w0, w1, w2, w3, out_ref):
    d_lat = jnp.sum(part_ref[...], axis=0)
    half = out_ref.shape[1]
    for i in range(out_ref.shape[0]):
        out_ref[i, :, : 2 * DH] = rows_ref[...]
        out_ref[i, :, 2 * DH : 3 * DH] = d_lat
        weights = (w0[i] + w1[i]) + (w2[i] + w3[i])
        out_ref[i, :, 3 * DH : 5 * DH] = weights[:half]
        out_ref[i, :, 5 * DH :] = weights[half:]


def gathered_kernel(got_ref, rows_ref):
    half = got_ref.shape[1]
    for i in range(got_ref.shape[0]):
        rows_ref[i * half : (i + 1) * half] = got_ref[i, :, : 3 * DH]


def weight_sum_kernel(mark_ref, got_ref, key_ref, value_ref, next_ref):
    half = got_ref.shape[1]
    total = got_ref[0, :, 3 * DH :]
    for i in range(1, got_ref.shape[0]):
        total += got_ref[i, :, 3 * DH :]
    key_ref[:half], key_ref[half:] = total[:, :DH], total[:, 2 * DH : 3 * DH]
    value_ref[:half], value_ref[half:] = total[:, DH : 2 * DH], total[:, 3 * DH :]
    next_ref[...] = mark_ref[...]


def final_kernel(y_ref, _, own, r1, r2, r3, lat_ref, dout_ref, d_lat_ref, d_wq_ref, d_wo_ref, all_rows):
    nz, rows = all_rows.shape[0], all_rows.shape[2]
    for k, part in enumerate((own, r1, r2, r3)):
        all_rows[:, lax.rem(y_ref[0] + NY - k, NY)] = part[...].reshape(nz, rows, 3 * DH)
    both = all_rows[...].reshape(d_lat_ref.shape[0], 3 * DH)
    d_lat_ref[...] = both[:, 2 * DH :]
    d_wq_ref[...] = dot3(lat_ref[...], both[:, :DH], 0, 0)
    d_wo_ref[...] = dot3(both[:, DH : 2 * DH], dout_ref[...], 0, 0)


def on_device(latents, observations, w_query, w_key, w_value, w_out, d_out):
    lat = latents.shape[0]
    width = observations.shape[1]
    n_ctx, n_head = lax.axis_size("ctx"), lax.axis_size("head")
    nz, nx = n_ctx // NY, n_head // 2
    ctx, head = lax.axis_index("ctx"), lax.axis_index("head")
    z, y = ctx // NY, ctx % NY
    x, core = head // 2, head % 2
    z_groups = [[a * NY + b for a in range(nz)] for b in range(NY)]
    swap = [(i, i ^ 1) for i in range(n_head)]
    right = [(i, (i + 2) % n_head) for i in range(n_head)]
    left = [(i, (i - 2) % n_head) for i in range(n_head)]
    rows_z = lat // n_ctx
    rows_y = rows_z * nz

    def along_y(k):
        return [(i, i - i % NY + (i + k) % NY) for i in range(n_ctx)]

    kv, q3, g3, sent, stat, given = forward(
        n_ctx, core.reshape(1), latents, d_out, w_query, w_out, w_key, w_value, observations
    )
    stats = lax.all_to_all(sent, "ctx", 0, 0)
    taken = lax.ppermute(given, "head", swap)
    w_chip, mark = small_call(
        chip_weights_kernel, [shape(nx, 2 * DH, 4 * DH, dtype=BF16), shape(8, DH)],
        [w_key, w_value, taken], [jnp.stack([x, core])], name="chip_weights",
    )
    own, rows = token_grads(mark, stats, kv, q3, g3)

    half = own.shape[0] // 2
    other = lax.ppermute(own, "head", swap)
    rows = lax.all_to_all(rows.reshape(n_ctx, rows_z, 2 * DH), "ctx", 0, 0)
    d_w = weight_grads(y.reshape(1), nz, observations, own)
    d_w = [d_w[0]] + [lax.ppermute(d_w[k], "ctx", along_y(k)) for k in range(1, NY)]
    right_1, left_1 = token_part(
        first_kernel, own, other, w_chip, (2, 1, 3), [shape(2, half, DH)] * 2, "token_first", 60
    )
    from_left_1 = lax.ppermute(right_1, "head", right)
    from_right_1 = lax.ppermute(left_1, "head", left)
    near, back, home = token_part(
        rest_kernel, own, other, w_chip, (0, 1, 3),
        [shape(half, DH), shape(half, DH), shape(2, half, DH)], "token_rest", 24,
    )

    rows, part = loaded_call(
        latent_part_kernel, [shape(rows_z, 2 * DH), shape(n_head, rows_z, DH)],
        [rows, w_query], [], name="latent_part",
    )
    part = lax.all_to_all(part, "head", 0, 0)
    (sent,) = small_call(
        latent_rows_kernel, [shape(nz, rows_z, 7 * DH)], [rows, part, *d_w], [],
        name="latent_rows",
    )
    got = lax.all_to_all(sent, "ctx", 0, 0, axis_index_groups=z_groups)
    right_2, left_2 = small_call(
        second_kernel, [shape(half, DH)] * 2, [near, back, from_left_1, from_right_1], [],
        name="token_second",
    )
    from_left_2 = lax.ppermute(right_2, "head", right)
    from_right_2 = lax.ppermute(left_2, "head", left)
    (rows,) = small_call(
        gathered_kernel, [shape(rows_y, 3 * DH)], [got], [], name="gathered"
    )
    rows = [rows] + [lax.ppermute(rows, "ctx", along_y(k)) for k in range(1, NY)]
    d_observations, mark = small_call(
        last_kernel, [shape(2 * half, DH), shape(8, DH)],
        [home, from_left_1, from_right_1, from_left_2, from_right_2], [], name="token_last",
    )
    d_w_key, d_w_value, mark = small_call(
        weight_sum_kernel,
        [shape(width // n_ctx, DH), shape(width // n_ctx, DH), shape(8, DH)],
        [mark, got], [], name="weight_sum",
    )
    d_latents, d_w_query, d_w_out = small_call(
        final_kernel, [shape(lat, DH), shape(width, DH), shape(DH, width)],
        [mark, *rows, latents, d_out], [y.reshape(1)],
        scratch=[VMEM((nz, NY, rows_z, 3 * DH), F32)], name="final",
    )
    return (d_latents, d_observations, d_w_query, d_w_key, d_w_value, d_w_out)


def solution(mesh):
    placed = (
        P(),
        P("ctx", None),
        P(None, "head"),
        P(None, "head"),
        P(None, "head"),
        P("head", None),
        P(),
    )
    return jax.shard_map(
        on_device,
        mesh=mesh,
        in_specs=placed,
        out_specs=(
            P(None, "head"),
            P("ctx", "head"),
            P(None, "head"),
            P("ctx", "head"),
            P("ctx", "head"),
            P("head", None),
        ),
        check_vma=False,
    )
```
